1024 devices in a mesh: dp: 32 (over y_hi, x, core), seq: 32 (over z, y_lo).
Axes of the slice: x: 8, y: 8 (y_hi: 2, y_lo: 4; y = y_hi * 4 + y_lo), z: 8, core: 2. Of those that a mesh axis runs over, the one named last changes fastest.
Arguments:
- queries: bfloat16 [32, 512, 2048], P('dp', 'seq'), may hold values from -2 to 2
- enc_keys: bfloat16 [32, 4096, 2048], P('dp', 'seq'), may hold values from -1 to 1
- enc_values: bfloat16 [32, 4096, 2048], P('dp', 'seq'), may hold values from -0.375 to 0.375
- grad_context: bfloat16 [32, 512, 2048], P('dp', 'seq'), may hold values from -512 to 512
- enc_lengths: int32 [32], P('dp'), may hold values from 512 to 4096, as said below
Outputs:
- query_grad: bfloat16 [32, 512, 2048], P('dp', 'seq')
- key_grad: bfloat16 [32, 4096, 2048], P('dp', 'seq')
- value_grad: bfloat16 [32, 4096, 2048], P('dp', 'seq')
The draws below stay inside these ranges and needn't reach their ends.
Inputs may be any that keep to these rules, and one draw needn't show every extreme that they name: `enc_lengths`: at least 512 live positions; some example has all 4096.
All inputs are finite; a program needn't handle non-finite values.
Results may differ from the reference program's by a relative error of at most 0.035.
Values may be sent and summed in bfloat16 or wider, within the bound.
A program may use at most 64 MiB of HBM per device.

```python
import jax
import jax.numpy as jnp
from jax import lax

HEADS = 8
HEAD_DIM = 256
ENC_LEN = 4096
DEC_LEN = 512
BATCH = 32
WIDTH = 2048


def joint_fields(key):
    folded = jax.random.fold_in(key, 17)
    subkeys = jax.random.split(folded, 8)
    width = HEADS * HEAD_DIM
    grad_scale = float(ENC_LEN // 32)
    queries = 0.25 * jnp.clip(jax.random.normal(subkeys[0], (BATCH, DEC_LEN, width), jnp.float32), -4.0, 4.0)
    key_rows = 0.25 * jnp.clip(jax.random.normal(subkeys[2], (BATCH, ENC_LEN, width), jnp.float32), -4.0, 4.0)
    gradients = grad_scale * jnp.clip(jax.random.normal(subkeys[3], (BATCH, DEC_LEN, width), jnp.float32), -4.0, 4.0)
    query_scale = float(512 // HEAD_DIM)
    sign_row = jnp.where(jax.random.bernoulli(subkeys[4], 0.5, (BATCH, 1, width)), 1.0, -1.0)
    anchor = jax.random.randint(subkeys[5], (BATCH, 1, 1), 0, ENC_LEN // 8 - 1)
    key_index = jnp.arange(ENC_LEN, dtype=jnp.int32).reshape(1, ENC_LEN, 1)
    column = jnp.arange(width, dtype=jnp.int32).reshape(1, 1, width)
    lowered = jnp.where(column % HEAD_DIM == 0, sign_row * (1.0 - 2.0 / query_scale), sign_row)
    key_rows = jnp.where(key_index == anchor, sign_row, key_rows)
    key_rows = jnp.where(key_index == anchor + 1, lowered, key_rows)
    base_row = jax.random.randint(subkeys[6], (BATCH, 1, 1), 0, DEC_LEN)
    spacing = DEC_LEN // 4
    query_index = jnp.arange(DEC_LEN, dtype=jnp.int32).reshape(1, DEC_LEN, 1)
    free_signs = jnp.where(jax.random.bernoulli(subkeys[7], 0.5, (BATCH, 1, width)), 1.0, -1.0)
    broad = query_index == (base_row + 3 * spacing) % DEC_LEN
    queries = jnp.where(broad, query_scale * free_signs, queries)
    for slot_number, strength in enumerate((0.75, 0.875, 1.0)):
        aligned = query_index == (base_row + slot_number * spacing) % DEC_LEN
        queries = jnp.where(aligned, strength * query_scale * sign_row, queries)
        gradients = jnp.where(aligned, 0.02 * gradients, gradients)
    return (queries, key_rows, gradients)


def draw_queries(key, part):
    return joint_fields(key)[0].astype(jnp.bfloat16)


def draw_enc_keys(key, part):
    return joint_fields(key)[1].astype(jnp.bfloat16)


def draw_grad_context(key, part):
    return joint_fields(key)[2].astype(jnp.bfloat16)


def draw_enc_lengths(key, part):
    folded = jax.random.fold_in(key, 29)
    subkeys = jax.random.split(folded, 2)
    lengths = jax.random.randint(subkeys[0], (BATCH,), ENC_LEN // 8, ENC_LEN + 1)
    picked = jax.random.randint(subkeys[1], (), 0, BATCH)
    return jnp.where(jnp.arange(BATCH, dtype=jnp.int32) == picked, ENC_LEN, lengths).astype(jnp.int32)


def steps_of(stream_key, shape, shards, least, top_value):
    def one(position, blocks):
        draws = jax.random.uniform(jax.random.fold_in(jax.random.fold_in(stream_key, 6), position), (blocks,), jnp.float32, least / len(shards), top_value / len(shards))
        return jnp.repeat(jnp.exp(draws), shape[position] // blocks).reshape((-1,) + (1,) * (len(shape) - position - 1))

    gain = one(*shards[0])
    for cut in shards[1:]:
        gain = gain * one(*cut)
    return gain


def bell_draw(rng, extent, spread, bound, pieces=(), held_as=jnp.bfloat16):
    array = jax.random.normal(rng, extent, jnp.float32) * spread
    if len(pieces) > 0:
        array = steps_of(rng, extent, pieces, -0.22, 0.18) * array
    return jnp.clip(array, min=-bound, max=bound).astype(held_as)


def setup_inputs(seed: int = 0) -> dict:
    seeds = jax.random.split(jax.random.key(seed), 6)
    return {
        "queries": draw_queries(jax.random.fold_in(seeds[5], 71), 0),
        "enc_keys": draw_enc_keys(jax.random.fold_in(seeds[5], 71), 0),
        "enc_values": bell_draw(seeds[2], (BATCH, ENC_LEN, WIDTH), HEAD_DIM ** -0.5, 0.375, ((0, 32), (1, 32))),
        "grad_context": draw_grad_context(jax.random.fold_in(seeds[5], 71), 0),
        "enc_lengths": draw_enc_lengths(jax.random.fold_in(seeds[5], 71), 0),
    }


def one_example(inputs):
    queries, enc_keys, enc_values, grad_context, length = inputs
    query_heads = queries.astype(jnp.float32).reshape(DEC_LEN, HEADS, HEAD_DIM)
    key_heads = enc_keys.astype(jnp.float32).reshape(ENC_LEN, HEADS, HEAD_DIM)
    value_heads = enc_values.astype(jnp.float32).reshape(ENC_LEN, HEADS, HEAD_DIM)
    grad_heads = grad_context.astype(jnp.float32).reshape(DEC_LEN, HEADS, HEAD_DIM)
    scores = jnp.einsum('qhd,khd->hqk', query_heads, key_heads)
    live_keys = jnp.arange(ENC_LEN, dtype=jnp.int32) < length
    masked = jnp.where(live_keys, scores, -jnp.inf)
    largest = jnp.max(masked, -1, keepdims=True)
    totals = jnp.sum(jnp.exp(masked - largest), -1, keepdims=True)
    log_total = largest + jnp.log(totals)
    weights = jnp.where(live_keys, jnp.exp(scores - log_total), jnp.float32(0.0))
    weight_grad = jnp.einsum('qhd,khd->hqk', grad_heads, value_heads)
    row_dots = jnp.sum(weights * weight_grad, -1, keepdims=True)
    score_grad = lax.optimization_barrier((weights * (weight_grad - row_dots)).astype(jnp.bfloat16)).astype(jnp.float32)
    weights_low = lax.optimization_barrier(weights.astype(jnp.bfloat16)).astype(jnp.float32)
    value_grad = jnp.einsum('hqk,qhd->khd', weights_low, grad_heads).astype(jnp.bfloat16)
    key_grad = jnp.einsum('hqk,qhd->khd', score_grad, query_heads).astype(jnp.bfloat16)
    query_grad = jnp.einsum('hqk,khd->qhd', score_grad, key_heads).astype(jnp.bfloat16)
    return (query_grad.reshape(DEC_LEN, WIDTH), key_grad.reshape(ENC_LEN, WIDTH), value_grad.reshape(ENC_LEN, WIDTH))


def reference(queries, enc_keys, enc_values, grad_context, enc_lengths):
    query_grad, key_grad, value_grad = lax.map(one_example, (queries, enc_keys, enc_values, grad_context, enc_lengths))
    return (query_grad, key_grad, value_grad)
```

```python
import functools

import jax
import jax.numpy as jnp
from jax import lax
from jax.experimental import pallas as pl
from jax.experimental.pallas import tpu as pltpu
from jax.sharding import PartitionSpec as P

HEADS = 8
NZ = 8
NY = 4
MESH = pl.DeviceIdType.MESH
NEAR_FIRST = (1, 7, 2, 6, 3, 5, 4)
FAR_FIRST = (4, 3, 5, 2, 6, 1, 7)
DEAD = -1e30
FLOOR = -1e20


def nt(a, b):
    return lax.dot_general(a, b, (((1,), (1,)), ((), ())), preferred_element_type=jnp.float32)


def tn(a, b):
    return lax.dot_general(a, b, (((0,), (0,)), ((), ())), preferred_element_type=jnp.float32)


def kernel(
    len_ref, q_ref, k_ref, v_ref, g_ref,
    dq_ref, dk_ref, dv_ref,
    qb, gb, kb, vb, pb, wb, sb, dkb, dvb, dqb, dqr, dqz, mlo, mli, rdo, rdi,
    z_send, z_recv, y_send, y_recv, own,
):
    seq = lax.axis_index("seq")
    z, y = seq // NY, seq % NY
    enc, dim = kb.shape[1], kb.shape[2]
    rows = q_ref.shape[0]
    block = NZ * rows
    lanes = mlo.shape[1]
    dec = NY * block

    def zpeer(d):
        return ((z + d) % NZ) * NY + y

    def ypeer(e):
        return z * NY + (y + e) % NY

    def cols(head):
        return pl.ds(pl.multiple_of((head % NZ) * dim, dim), dim)

    def remote(src, dst, send, recv, peer):
        return pltpu.make_async_remote_copy(
            src_ref=src, dst_ref=dst, send_sem=send, recv_sem=recv,
            device_id={"seq": peer}, device_id_type=MESH,
        )

    started = []

    def go(copy):
        copy.start()
        started.append(copy)
        return copy

    here = [
        pltpu.make_async_copy(q_ref.at[:, cols(z)], qb.at[pl.ds(0, rows)], own.at[0]),
        pltpu.make_async_copy(g_ref.at[:, cols(z)], gb.at[pl.ds(0, rows)], own.at[1]),
        pltpu.make_async_copy(k_ref.at[:, cols(z)], kb.at[0], own.at[2]),
        pltpu.make_async_copy(v_ref.at[:, cols(z)], vb.at[0], own.at[3]),
    ]
    for copy in here:
        copy.start()

    barrier = pltpu.get_barrier_semaphore()
    for d in range(1, NZ):
        pl.semaphore_signal(barrier, inc=1, device_id={"seq": zpeer(d)}, device_id_type=MESH)
    for e in range(1, NY):
        pl.semaphore_signal(barrier, inc=1, device_id={"seq": ypeer(e)}, device_id_type=MESH)
    pl.semaphore_wait(barrier, NZ - 1 + NY - 1)

    def z_out(kind, src, dst_at, order):
        return {
            d: go(remote(src.at[:, cols(z + d)], dst_at(d), z_send.at[kind, d], z_recv.at[kind, d], zpeer(d)))
            for d in order
        }

    q_in = z_out(0, q_ref, lambda d: qb.at[pl.ds(d * rows, rows)], FAR_FIRST)
    g_in = z_out(1, g_ref, lambda d: gb.at[pl.ds(d * rows, rows)], FAR_FIRST)
    k_in = z_out(2, k_ref, lambda d: kb.at[d], FAR_FIRST)

    def y_out(kind, buf):
        return {
            e: go(remote(
                buf.at[pl.ds(0, block)], buf.at[pl.ds(e * block, block)],
                y_send.at[kind, e], y_recv.at[kind, e], ypeer(e),
            ))
            for e in range(1, NY)
        }

    here[0].wait()
    for d in NEAR_FIRST:
        q_in[d].wait_recv()
    q_all = y_out(0, qb)
    here[1].wait()
    for d in NEAR_FIRST:
        g_in[d].wait_recv()
    g_all = y_out(1, gb)
    v_in = z_out(3, v_ref, lambda d: vb.at[d], FAR_FIRST)

    for e in range(1, NY):
        q_all[e].wait_recv()

    length = len_ref[0]
    tops, sums = [None] * NZ, [None] * NZ
    for d in (0,) + NEAR_FIRST:
        if d == 0:
            here[2].wait()
        else:
            k_in[d].wait_recv()
        scores = nt(kb[d], qb[...])
        base = (((z - d + NZ) % NZ) * NY + y) * enc
        live = base + lax.broadcasted_iota(jnp.int32, (enc, dec), 0) < length
        scores = jnp.where(live, scores, DEAD)
        top = jnp.maximum(jnp.max(scores, axis=0, keepdims=True), FLOOR)
        powers = jnp.exp(scores - top)
        tops[d], sums[d] = top, jnp.sum(powers, axis=0, keepdims=True)
        pb[d] = powers

    top = functools.reduce(jnp.maximum, tops)
    total = functools.reduce(jnp.add, [s * jnp.exp(t - top) for s, t in zip(sums, tops)])
    for i in range(NY):
        mlo[i : i + 1, :] = top[:, i * lanes : (i + 1) * lanes]
        mlo[NY + i : NY + i + 1, :] = total[:, i * lanes : (i + 1) * lanes]

    ml = {
        e: go(remote(mlo, mli.at[e], y_send.at[2, e], y_recv.at[2, e], ypeer(e)))
        for e in range(1, NY)
    }

    def arrived(buf, e, first):
        at = [first + (i - e) % NY for i in range(NY)]
        return jnp.concatenate([buf[e, r : r + 1, :] for r in at], axis=1)

    for e in range(1, NY):
        g_all[e].wait_recv()
    for e in range(1, NY):
        ml[e].wait_recv()
    all_tops = [top] + [arrived(mli, e, 0) for e in range(1, NY)]
    all_sums = [total] + [arrived(mli, e, NY) for e in range(1, NY)]
    largest = functools.reduce(jnp.maximum, all_tops)
    total = functools.reduce(jnp.add, [s * jnp.exp(t - largest) for s, t in zip(all_sums, all_tops)])
    share = 1.0 / total

    def z_back(kind, d, src, dst):
        return go(remote(
            src, dst.at[:, cols(z)], z_send.at[kind, d], z_recv.at[kind, d], zpeer(NZ - d),
        ))

    dv_in, dk_in, dq_in = {}, {}, {}
    for d in FAR_FIRST + (0,):
        weights = pb[d] * (jnp.exp(tops[d] - largest) * share)
        pb[d] = weights
        grad = jnp.dot(weights.astype(jnp.bfloat16), gb[...], preferred_element_type=jnp.float32)
        dvb[d] = grad.astype(jnp.bfloat16)
        if d:
            dv_in[d] = z_back(4, d, dvb.at[d], dv_ref)
    dv_own = pltpu.make_async_copy(dvb.at[0], dv_ref.at[:, cols(z)], own.at[4])
    dv_own.start()

    dots = jnp.zeros((1, dec), jnp.float32)
    for d in (0,) + NEAR_FIRST:
        if d == 0:
            here[3].wait()
        else:
            v_in[d].wait_recv()
        weight_grad = nt(vb[d], gb[...])
        wb[d] = weight_grad
        dots = dots + jnp.sum(pb[d] * weight_grad, axis=0, keepdims=True)
    rdo[...] = jnp.zeros_like(rdo)
    for i in range(NY):
        rdo[i : i + 1, :] = dots[:, i * lanes : (i + 1) * lanes]
    rd = {
        e: go(remote(rdo, rdi.at[e], y_send.at[3, e], y_recv.at[3, e], ypeer(e)))
        for e in range(1, NY)
    }
    for e in range(1, NY):
        rd[e].wait_recv()
    for e in range(1, NY):
        dots = dots + arrived(rdi, e, 0)

    for d in range(NZ):
        sb[pl.ds(d * enc, enc), :] = (pb[d] * (wb[d] - dots)).astype(jnp.bfloat16)

    keys = kb[...].reshape(NZ * enc, dim)
    dq_y = {}
    for e in range(1, NY):
        part = tn(sb[:, e * block : (e + 1) * block], keys)
        dqb[e] = part.astype(jnp.bfloat16)
        dq_y[e] = go(remote(dqb.at[e], dqr.at[e], y_send.at[4, e], y_recv.at[4, e], ypeer(NY - e)))
    mine = tn(sb[:, 0:block], keys)

    for d in FAR_FIRST + (0,):
        grad = jnp.dot(sb[pl.ds(d * enc, enc), :], qb[...], preferred_element_type=jnp.float32)
        dkb[d] = grad.astype(jnp.bfloat16)
        if d:
            dk_in[d] = z_back(5, d, dkb.at[d], dk_ref)
    dk_own = pltpu.make_async_copy(dkb.at[0], dk_ref.at[:, cols(z)], own.at[5])
    dk_own.start()

    for e in range(1, NY):
        dq_y[e].wait_recv()
        mine = mine + dqr[e].astype(jnp.float32)
    dqz[...] = mine.astype(jnp.bfloat16)
    for d in FAR_FIRST:
        dq_in[d] = z_back(6, d, dqz.at[pl.ds(d * rows, rows)], dq_ref)
    dq_own = pltpu.make_async_copy(dqz.at[pl.ds(0, rows)], dq_ref.at[:, cols(z)], own.at[6])
    dq_own.start()

    for copy in (dv_own, dk_own, dq_own):
        copy.wait()
    for group in (dv_in, dk_in, dq_in):
        for d in NEAR_FIRST:
            group[d].wait_recv()
    for copy in started:
        copy.wait_send()


def body(queries, enc_keys, enc_values, grad_context, enc_lengths):
    rows, width = queries.shape[1:]
    enc = enc_keys.shape[1]
    dim = width // HEADS
    block = NZ * rows
    dec = NY * block
    any_spec = pl.BlockSpec(memory_space=pl.ANY)
    bf16, f32 = jnp.bfloat16, jnp.float32
    dq, dk, dv = pl.pallas_call(
        kernel,
        out_shape=(
            jax.ShapeDtypeStruct((rows, width), bf16),
            jax.ShapeDtypeStruct((enc, width), bf16),
            jax.ShapeDtypeStruct((enc, width), bf16),
        ),
        in_specs=[pl.BlockSpec(memory_space=pltpu.SMEM)] + [any_spec] * 4,
        out_specs=(any_spec,) * 3,
        scratch_shapes=[
            pltpu.VMEM((dec, dim), bf16),
            pltpu.VMEM((dec, dim), bf16),
            pltpu.VMEM((NZ, enc, dim), bf16),
            pltpu.VMEM((NZ, enc, dim), bf16),
            pltpu.VMEM((NZ, enc, dec), f32),
            pltpu.VMEM((NZ, enc, dec), f32),
            pltpu.VMEM((NZ * enc, dec), bf16),
            pltpu.VMEM((NZ, enc, dim), bf16),
            pltpu.VMEM((NZ, enc, dim), bf16),
            pltpu.VMEM((NY, block, dim), bf16),
            pltpu.VMEM((NY, block, dim), bf16),
            pltpu.VMEM((block, dim), bf16),
            pltpu.VMEM((2 * NY, dec // NY), f32),
            pltpu.VMEM((NY, 2 * NY, dec // NY), f32),
            pltpu.VMEM((2 * NY, dec // NY), f32),
            pltpu.VMEM((NY, 2 * NY, dec // NY), f32),
            pltpu.SemaphoreType.DMA((7, NZ)),
            pltpu.SemaphoreType.DMA((7, NZ)),
            pltpu.SemaphoreType.DMA((5, NY)),
            pltpu.SemaphoreType.DMA((5, NY)),
            pltpu.SemaphoreType.DMA((7,)),
        ],
        compiler_params=pltpu.CompilerParams(
            collective_id=0, has_side_effects=True, vmem_limit_bytes=32 * 1024 * 1024
        ),
        cost_estimate=pl.CostEstimate(
            flops=10 * NZ * enc * dec * dim,
            bytes_accessed=8 * enc * width + 6 * rows * width,
            transcendentals=NZ * enc * dec,
        ),
    )(enc_lengths, queries[0], enc_keys[0], enc_values[0], grad_context[0])
    return (dq[None], dk[None], dv[None])


def solution(mesh):
    spec = P("dp", "seq", None)
    return jax.shard_map(
        body,
        mesh=mesh,
        in_specs=(spec, spec, spec, spec, P("dp")),
        out_specs=(spec, spec, spec),
        check_vma=False,
    )
```

```python
import functools

import jax
import jax.numpy as jnp
from jax import lax
from jax.experimental import pallas as pl
from jax.experimental.pallas import tpu as pltpu
from jax.sharding import PartitionSpec as P

HEADS = 8
NZ = 8
NY = 4
GZ = 4
MESH = pl.DeviceIdType.MESH
DEAD = -1e30
FLOOR = -1e20
PIECES = ((2, 1), (-2, 1), (1, 1), (-1, 1), (2, 0), (-2, 0), (1, 0), (-1, 0), (0, 1))
CHUNK = {0: 0, 1: 1, -1: 2, 2: 3, -2: 3}
NEAR = (4, 3, 5, 2, 6, 1, 7)


def nt(a, b):
    return lax.dot_general(a, b, (((1,), (1,)), ((), ())), preferred_element_type=jnp.float32)


def tn(a, b):
    return lax.dot_general(a, b, (((0,), (0,)), ((), ())), preferred_element_type=jnp.float32)


def kernel(
    len_ref, q_hbm, k_hbm, v_hbm, g_hbm,
    dq_ref, dk_ref, dv_ref,
    q_ref, k_ref, v_ref, g_ref, dqo, dko, dvo,
    qz, gz, qb, gb, kb, vb, pb, wb, sb, dkb, dvb, dqb, dqy, dqz, dqr, mlo, mli, rdo, rdi,
    z_send, z_recv, y_send, y_recv, p_send, p_recv, s_send, s_recv, own,
):
    seq = lax.axis_index("seq")
    z, y = seq // NY, seq % NY
    rows = q_ref.shape[0]
    enc = k_ref.shape[0]
    dim = kb.shape[2]
    block = NZ * rows
    dec = NY * block
    lanes = mlo.shape[1]
    half = enc // 2
    side = y % 2
    other = y + 1 - 2 * side

    def device(dz, at_y):
        return ((z + dz + NZ) % NZ) * NY + at_y

    def zpeer(d):
        return device(d, y)

    def ypeer(e):
        return z * NY + (y + e) % NY

    def cols(dz, at_y):
        head = 2 * ((z + dz + NZ) % GZ) + at_y % 2
        return pl.ds(pl.multiple_of(head * dim, dim), dim)

    def pair(dz):
        return pl.ds(pl.multiple_of(((z + dz + NZ) % GZ) * (2 * dim), 2 * dim), 2 * dim)

    def half_of(at_y):
        return pl.ds(pl.multiple_of((at_y % 2) * dim, dim), dim)

    def part(dz):
        return {2: pl.ds(0, half), -2: pl.ds(half, half)}.get(dz, pl.ds(0, enc))

    def remote(src, dst, send, recv, peer):
        return pltpu.make_async_remote_copy(
            src_ref=src, dst_ref=dst, send_sem=send, recv_sem=recv,
            device_id={"seq": peer}, device_id_type=MESH,
        )

    started = []

    def go(copy):
        copy.start()
        started.append(copy)
        return copy

    loads = [
        pltpu.make_async_copy(src, dst, own.at[i])
        for i, (src, dst) in enumerate(((q_hbm, q_ref), (g_hbm, g_ref), (k_hbm, k_ref), (v_hbm, v_ref)))
    ]
    for copy in loads:
        copy.start()

    barrier = pltpu.get_barrier_semaphore()
    peers = [zpeer(d) for d in range(1, NZ)] + [ypeer(e) for e in range(1, NY)]
    peers += [device(dz, other) for dz in (1, -1, 2, -2)] + [device(4, (y + 2) % NY)]
    for peer in peers:
        pl.semaphore_signal(barrier, inc=1, device_id={"seq": peer}, device_id_type=MESH)
    pl.semaphore_wait(barrier, len(peers))

    def z_out(kind, src, into):
        return {
            d: go(remote(
                src.at[:, pair(d)], into.at[pl.ds(d * rows, rows)], z_send.at[kind, d], z_recv.at[kind, d], zpeer(d),
            ))
            for d in NEAR
        }

    def y_out(kind, src, into):
        return {
            e: go(remote(
                src.at[:, half_of(y + e)], into.at[pl.ds(e * block, block)],
                y_send.at[kind, e], y_recv.at[kind, e], ypeer(e),
            ))
            for e in (2, 3, 1)
        }

    def p_out(kind, src, into):
        out = {}
        for i, (dz, turn) in enumerate(PIECES):
            at_y = other if turn else y
            at = into.at[4 * turn + CHUNK[dz], part(dz)] if dz in (2, -2) else into.at[4 * turn + CHUNK[dz]]
            out[dz, turn] = go(remote(
                src.at[part(dz), cols(dz, at_y)], at, p_send.at[kind, i], p_recv.at[kind, i], device(dz, at_y),
            ))
        return out

    loads[0].wait()
    q_in = z_out(0, q_ref, qz)
    loads[1].wait()
    g_in = z_out(1, g_ref, gz)
    loads[2].wait()
    k_in = p_out(0, k_ref, kb)
    loads[3].wait()

    qz[0:rows, :] = q_ref[:, pair(0)]
    gz[0:rows, :] = g_ref[:, pair(0)]
    for d in reversed(NEAR):
        q_in[d].wait_recv()
    q_all = y_out(0, qz, qb)
    for d in reversed(NEAR):
        g_in[d].wait_recv()
    g_all = y_out(1, gz, gb)
    v_in = p_out(1, v_ref, vb)

    qb[0:block, :] = qz[:, half_of(y)]
    gb[0:block, :] = gz[:, half_of(y)]
    kb[0] = k_ref[:, cols(0, y)]
    vb[0] = v_ref[:, cols(0, y)]
    for e in range(1, NY):
        q_all[e].wait_recv()

    def arrive(copies, c):
        turn, i = divmod(c, 4)
        for dz in ((0,), (1,), (-1,), (2, -2))[i]:
            if (dz, turn) in copies:
                copies[dz, turn].wait_recv()

    order = (0, 4, 1, 2, 5, 6, 3, 7)

    length = len_ref[0]
    row = lax.broadcasted_iota(jnp.int32, (enc, dec), 0)
    tops, sums = [None] * 8, [None] * 8
    for c in order:
        arrive(k_in, c)
        turn, i = divmod(c, 4)
        at_y = other if turn else y

        def base(dz):
            return (((z + dz + NZ) % NZ) * NY + at_y) * enc

        first = (0, -1, 1, -2)[i]
        live = row + base(first) < length
        if i == 3:
            live = jnp.where(row < half, row + base(-2), row + base(2)) < length
        scores = jnp.where(live, nt(kb[c], qb[...]), DEAD)
        top = jnp.maximum(jnp.max(scores, axis=0, keepdims=True), FLOOR)
        powers = jnp.exp(scores - top)
        tops[c], sums[c] = top, jnp.sum(powers, axis=0, keepdims=True)
        pb[c] = powers

    shared = (device(4, y), device(0, (y + 2) % NY), device(4, (y + 2) % NY))
    turned = ((4, 0), (0, 2), (4, 2))

    def put(buf, at, values):
        for i in range(NY):
            buf[at + i : at + i + 1, :] = values[:, i * lanes : (i + 1) * lanes]

    def exchange(kind, out, into):
        return [
            go(remote(out, into.at[i], s_send.at[kind, i], s_recv.at[kind, i], shared[i]))
            for i in range(3)
        ]

    def take(buf, i, at):
        tile = buf[i]
        if turned[i][0]:
            tile = pltpu.roll(tile, lanes // 2, 1)
        return jnp.concatenate(
            [tile[at + (k + turned[i][1]) % NY : at + (k + turned[i][1]) % NY + 1, :] for k in range(NY)], axis=1
        )

    top = functools.reduce(jnp.maximum, tops)
    total = functools.reduce(jnp.add, [s * jnp.exp(t - top) for s, t in zip(sums, tops)])
    put(mlo, 0, top)
    put(mlo, NY, total)
    ml = exchange(0, mlo, mli)
    for e in range(1, NY):
        g_all[e].wait_recv()
    for copy in ml:
        copy.wait_recv()
    all_tops = [top] + [take(mli, i, 0) for i in range(3)]
    all_sums = [total] + [take(mli, i, NY) for i in range(3)]
    largest = functools.reduce(jnp.maximum, all_tops)
    total = functools.reduce(jnp.add, [s * jnp.exp(t - largest) for s, t in zip(all_sums, all_tops)])
    share = 1.0 / total

    dots = jnp.zeros((1, dec), jnp.float32)
    for c in order:
        arrive(v_in, c)
        weights = pb[c] * (jnp.exp(tops[c] - largest) * share)
        pb[c] = weights
        weight_grad = nt(vb[c], gb[...])
        wb[c] = weight_grad
        dots = dots + jnp.sum(weights * weight_grad, axis=0, keepdims=True)
    rdo[...] = jnp.zeros_like(rdo)
    put(rdo, 0, dots)
    rd = exchange(1, rdo, rdi)

    def give(kind, src, into, c):
        turn, i = divmod(c, 4)
        out = {}
        for dz in ((0,), (1,), (-1,), (2, -2))[i]:
            if (dz, turn) not in PIECES:
                into[:, cols(0, y)] = src[c]
                continue
            at_y = other if turn else y
            at = src.at[c, part(dz)] if dz in (2, -2) else src.at[c]
            n = PIECES.index((dz, turn))
            out[dz, turn] = go(remote(
                at, into.at[part(dz), cols(0, y)], p_send.at[kind, n], p_recv.at[kind, n], device(-dz, at_y),
            ))
        return out

    back = {2: {}, 3: {}}
    far_first = (7, 3, 5, 6, 1, 2, 4, 0)
    for c in far_first:
        grad = jnp.dot(pb[c].astype(jnp.bfloat16), gb[...], preferred_element_type=jnp.float32)
        dvb[c] = grad.astype(jnp.bfloat16)
        back[2].update(give(2, dvb, dvo, c))

    for copy in rd:
        copy.wait_recv()
    for i in range(3):
        dots = dots + take(rdi, i, 0)
    for c in range(8):
        sb[pl.ds(c * enc, enc), :] = (pb[c] * (wb[c] - dots)).astype(jnp.bfloat16)

    keys = kb[...].reshape(8 * enc, dim)
    dq_y = {}
    for e in (2, 3, 1):
        dqb[e] = tn(sb[:, e * block : (e + 1) * block], keys).astype(jnp.bfloat16)
        dq_y[e] = go(remote(dqb.at[e], dqy.at[e], y_send.at[2, e], y_recv.at[2, e], ypeer(NY - e)))
    mine = tn(sb[:, 0:block], keys)

    for c in far_first:
        grad = jnp.dot(sb[pl.ds(c * enc, enc), :], qb[...], preferred_element_type=jnp.float32)
        dkb[c] = grad.astype(jnp.bfloat16)
        back[3].update(give(3, dkb, dko, c))

    for e in range(1, NY):
        dq_y[e].wait_recv()
    mine = (mine + dqy[2].astype(jnp.float32)).astype(jnp.bfloat16)
    theirs = (dqy[1].astype(jnp.float32) + dqy[3].astype(jnp.float32)).astype(jnp.bfloat16)
    dqz[:, half_of(y)] = mine
    dqz[:, half_of(other)] = theirs
    dq_z = {
        d: go(remote(
            dqz.at[pl.ds(d * rows, rows)], dqr.at[d], z_send.at[2, d], z_recv.at[2, d], zpeer(NZ - d),
        ))
        for d in NEAR
    }
    dqr[0] = dqz[0:rows, :]

    for copy in back[2].values():
        copy.wait_recv()
    out_v = pltpu.make_async_copy(dvo, dv_ref, own.at[4])
    out_v.start()
    for copy in back[3].values():
        copy.wait_recv()
    out_k = pltpu.make_async_copy(dko, dk_ref, own.at[5])
    out_k.start()
    for d in range(1, NZ):
        dq_z[d].wait_recv()
    for d in range(GZ):
        dqo[:, pair(d)] = (dqr[d].astype(jnp.float32) + dqr[d + GZ].astype(jnp.float32)).astype(jnp.bfloat16)
    out_q = pltpu.make_async_copy(dqo, dq_ref, own.at[6])
    out_q.start()
    for copy in started:
        copy.wait_send()
    for copy in (out_v, out_k, out_q):
        copy.wait()


def settle(dq_from, dk_from, dv_from, dq_ref, dk_ref, dv_ref):
    dq_ref[...] = dq_from[...]
    dk_ref[...] = dk_from[...]
    dv_ref[...] = dv_from[...]


def body(queries, enc_keys, enc_values, grad_context, enc_lengths):
    rows, width = queries.shape[1:]
    enc = enc_keys.shape[1]
    dim = width // HEADS
    block = NZ * rows
    dec = NY * block
    lanes = dec // NY
    any_spec = pl.BlockSpec(memory_space=pl.ANY)
    bf16, f32 = jnp.bfloat16, jnp.float32
    vmem = pltpu.VMEM
    dma = pltpu.SemaphoreType.DMA
    outs = (
        jax.ShapeDtypeStruct((rows, width), bf16),
        jax.ShapeDtypeStruct((enc, width), bf16),
        jax.ShapeDtypeStruct((enc, width), bf16),
    )
    grads = pl.pallas_call(
        kernel,
        out_shape=outs,
        in_specs=[pl.BlockSpec(memory_space=pltpu.SMEM)] + [any_spec] * 4,
        out_specs=(any_spec,) * 3,
        scratch_shapes=[
            vmem((rows, width), bf16), vmem((enc, width), bf16),
            vmem((enc, width), bf16), vmem((rows, width), bf16),
            vmem((rows, width), bf16), vmem((enc, width), bf16), vmem((enc, width), bf16),
            vmem((block, 2 * dim), bf16), vmem((block, 2 * dim), bf16),
            vmem((dec, dim), bf16), vmem((dec, dim), bf16),
            vmem((8, enc, dim), bf16), vmem((8, enc, dim), bf16),
            vmem((8, enc, dec), f32), vmem((8, enc, dec), f32),
            vmem((8 * enc, dec), bf16),
            vmem((8, enc, dim), bf16), vmem((8, enc, dim), bf16),
            vmem((NY, block, dim), bf16), vmem((NY, block, dim), bf16),
            vmem((block, 2 * dim), bf16), vmem((NZ, rows, 2 * dim), bf16),
            vmem((2 * NY, lanes), f32), vmem((3, 2 * NY, lanes), f32),
            vmem((2 * NY, lanes), f32), vmem((3, 2 * NY, lanes), f32),
            dma((3, NZ)), dma((3, NZ)), dma((3, NY)), dma((3, NY)),
            dma((4, len(PIECES))), dma((4, len(PIECES))), dma((2, 3)), dma((2, 3)), dma((7,)),
        ],
        compiler_params=pltpu.CompilerParams(
            collective_id=0, has_side_effects=True, vmem_limit_bytes=56 * 1024 * 1024
        ),
        cost_estimate=pl.CostEstimate(
            flops=80 * enc * dec * dim,
            bytes_accessed=8 * enc * width + 6 * rows * width,
            transcendentals=8 * enc * dec,
        ),
    )(enc_lengths, queries[0], enc_keys[0], enc_values[0], grad_context[0])
    parts = 1
    specs = tuple(pl.BlockSpec((a.shape[0] // parts, width), lambda i: (i, 0)) for a in outs)
    dq, dk, dv = pl.pallas_call(settle, grid=(parts,), out_shape=outs, in_specs=specs, out_specs=specs)(*grads)
    return (dq[None], dk[None], dv[None])


def solution(mesh):
    spec = P("dp", "seq", None)
    return jax.shard_map(
        body,
        mesh=mesh,
        in_specs=(spec, spec, spec, spec, P("dp")),
        out_specs=(spec, spec, spec),
        check_vma=False,
    )
```

```python
import functools

import jax
import jax.numpy as jnp
from jax import lax
from jax.experimental import pallas as pl
from jax.experimental.pallas import tpu as pltpu
from jax.sharding import PartitionSpec as P

HEADS = 8
NZ = 8
NY = 4
GZ = 4
MESH = pl.DeviceIdType.MESH
DEAD = -1e30
FLOOR = -1e20
PIECES = ((2, 1), (-2, 1), (1, 1), (-1, 1), (2, 0), (-2, 0), (1, 0), (-1, 0), (0, 1))
CHUNK = {0: 0, 1: 1, -1: 2, 2: 3, -2: 3}
NEAR = (4, 3, 5, 2, 6, 1, 7)


def nt(a, b):
    return lax.dot_general(a, b, (((1,), (1,)), ((), ())), preferred_element_type=jnp.float32)


def tn(a, b):
    return lax.dot_general(a, b, (((0,), (0,)), ((), ())), preferred_element_type=jnp.float32)


def kernel(
    len_ref, q_hbm, k_hbm, v_hbm, g_hbm,
    dq_ref, dk_ref, dv_ref,
    q_ref, k_ref, v_ref, g_ref, dqo, dko, dvo,
    qz, gz, qb, gb, kb, vb, pb, wb, sb, dkb, dvb, dqb, dqy, dqz, dqr, mlo, mli, rdo, rdi,
    z_send, z_recv, y_send, y_recv, p_send, p_recv, s_send, s_recv, own,
):
    seq = lax.axis_index("seq")
    z, y = seq // NY, seq % NY
    rows = q_ref.shape[0]
    enc = k_ref.shape[0]
    dim = kb.shape[2]
    block = NZ * rows
    dec = NY * block
    lanes = mlo.shape[1]
    half = enc // 2
    side = y % 2
    other = y + 1 - 2 * side

    def device(dz, at_y):
        return ((z + dz + NZ) % NZ) * NY + at_y

    def zpeer(d):
        return device(d, y)

    def ypeer(e):
        return z * NY + (y + e) % NY

    def cols(dz, at_y):
        head = 2 * ((z + dz + NZ) % GZ) + at_y % 2
        return pl.ds(pl.multiple_of(head * dim, dim), dim)

    def pair(dz):
        return pl.ds(pl.multiple_of(((z + dz + NZ) % GZ) * (2 * dim), 2 * dim), 2 * dim)

    def half_of(at_y):
        return pl.ds(pl.multiple_of((at_y % 2) * dim, dim), dim)

    def part(dz):
        return {2: pl.ds(0, half), -2: pl.ds(half, half)}.get(dz, pl.ds(0, enc))

    def remote(src, dst, send, recv, peer):
        return pltpu.make_async_remote_copy(
            src_ref=src, dst_ref=dst, send_sem=send, recv_sem=recv,
            device_id={"seq": peer}, device_id_type=MESH,
        )

    started = []

    def go(copy):
        copy.start()
        started.append(copy)
        return copy

    loads = [
        pltpu.make_async_copy(src, dst, own.at[i])
        for i, (src, dst) in enumerate(((q_hbm, q_ref), (g_hbm, g_ref), (k_hbm, k_ref), (v_hbm, v_ref)))
    ]
    for copy in loads:
        copy.start()

    barrier = pltpu.get_barrier_semaphore()
    peers = [zpeer(d) for d in range(1, NZ)] + [ypeer(e) for e in range(1, NY)]
    peers += [device(dz, other) for dz in (1, -1, 2, -2)] + [device(4, (y + 2) % NY)]
    for peer in peers:
        pl.semaphore_signal(barrier, inc=1, device_id={"seq": peer}, device_id_type=MESH)
    pl.semaphore_wait(barrier, len(peers))

    def z_out(kind, src, into):
        return {
            d: go(remote(
                src.at[:, pair(d)], into.at[pl.ds(d * rows, rows)], z_send.at[kind, d], z_recv.at[kind, d], zpeer(d),
            ))
            for d in NEAR
        }

    def y_out(kind, src, into):
        return {
            e: go(remote(
                src.at[:, half_of(y + e)], into.at[pl.ds(e * block, block)],
                y_send.at[kind, e], y_recv.at[kind, e], ypeer(e),
            ))
            for e in (2, 3, 1)
        }

    def p_out(kind, src, into):
        out = {}
        for i, (dz, turn) in enumerate(PIECES):
            at_y = other if turn else y
            at = into.at[4 * turn + CHUNK[dz], part(dz)] if dz in (2, -2) else into.at[4 * turn + CHUNK[dz]]
            out[dz, turn] = go(remote(
                src.at[part(dz), cols(dz, at_y)], at, p_send.at[kind, i], p_recv.at[kind, i], device(dz, at_y),
            ))
        return out

    loads[0].wait()
    q_in = z_out(0, q_ref, qz)
    loads[1].wait()
    g_in = z_out(1, g_ref, gz)
    loads[2].wait()
    k_in = p_out(0, k_ref, kb)
    loads[3].wait()

    qz[0:rows, :] = q_ref[:, pair(0)]
    gz[0:rows, :] = g_ref[:, pair(0)]
    for d in reversed(NEAR):
        q_in[d].wait_recv()
    q_all = y_out(0, qz, qb)
    for d in reversed(NEAR):
        g_in[d].wait_recv()
    g_all = y_out(1, gz, gb)
    v_in = p_out(1, v_ref, vb)

    qb[0:block, :] = qz[:, half_of(y)]
    gb[0:block, :] = gz[:, half_of(y)]
    kb[0] = k_ref[:, cols(0, y)]
    vb[0] = v_ref[:, cols(0, y)]
    for e in range(1, NY):
        q_all[e].wait_recv()

    def arrive(copies, c):
        turn, i = divmod(c, 4)
        for dz in ((0,), (1,), (-1,), (2, -2))[i]:
            if (dz, turn) in copies:
                copies[dz, turn].wait_recv()

    order = (0, 4, 1, 2, 5, 6, 3, 7)

    length = len_ref[0]
    row = lax.broadcasted_iota(jnp.int32, (enc, dec), 0)
    tops, sums = [None] * 8, [None] * 8
    for c in order:
        arrive(k_in, c)
        turn, i = divmod(c, 4)
        at_y = other if turn else y

        def base(dz):
            return (((z + dz + NZ) % NZ) * NY + at_y) * enc

        first = (0, -1, 1, -2)[i]
        live = row + base(first) < length
        if i == 3:
            live = jnp.where(row < half, row + base(-2), row + base(2)) < length
        scores = jnp.where(live, nt(kb[c], qb[...]), DEAD)
        top = jnp.maximum(jnp.max(scores, axis=0, keepdims=True), FLOOR)
        powers = jnp.exp(scores - top)
        tops[c], sums[c] = top, jnp.sum(powers, axis=0, keepdims=True)
        pb[c] = powers

    shared = (device(4, y), device(0, (y + 2) % NY), device(4, (y + 2) % NY))
    turned = ((4, 0), (0, 2), (4, 2))

    def put(buf, at, values):
        for i in range(NY):
            buf[at + i : at + i + 1, :] = values[:, i * lanes : (i + 1) * lanes]

    def exchange(kind, out, into):
        return [
            go(remote(out, into.at[i], s_send.at[kind, i], s_recv.at[kind, i], shared[i]))
            for i in range(3)
        ]

    def take(buf, i, at):
        tile = buf[i]
        if turned[i][0]:
            tile = pltpu.roll(tile, lanes // 2, 1)
        return jnp.concatenate(
            [tile[at + (k + turned[i][1]) % NY : at + (k + turned[i][1]) % NY + 1, :] for k in range(NY)], axis=1
        )

    top = functools.reduce(jnp.maximum, tops)
    total = functools.reduce(jnp.add, [s * jnp.exp(t - top) for s, t in zip(sums, tops)])
    put(mlo, 0, top)
    put(mlo, NY, total)
    ml = exchange(0, mlo, mli)
    for e in range(1, NY):
        g_all[e].wait_recv()

    dots = jnp.zeros((1, dec), jnp.float32)
    for c in order:
        arrive(v_in, c)
        weight_grad = nt(vb[c], gb[...])
        wb[c] = weight_grad
        dots = dots + jnp.sum(pb[c] * weight_grad, axis=0, keepdims=True) * jnp.exp(tops[c] - top)
    rdo[...] = jnp.zeros_like(rdo)
    put(rdo, 0, dots)
    rd = exchange(1, rdo, rdi)

    for copy in ml:
        copy.wait_recv()
    all_tops = [top] + [take(mli, i, 0) for i in range(3)]
    all_sums = [total] + [take(mli, i, NY) for i in range(3)]
    largest = functools.reduce(jnp.maximum, all_tops)
    scales = [jnp.exp(t - largest) for t in all_tops]
    share = 1.0 / functools.reduce(jnp.add, [s * r for s, r in zip(all_sums, scales)])

    def give(kind, src, into, c):
        turn, i = divmod(c, 4)
        out = {}
        for dz in ((0,), (1,), (-1,), (2, -2))[i]:
            if (dz, turn) not in PIECES:
                into[:, cols(0, y)] = src[c]
                continue
            at_y = other if turn else y
            at = src.at[c, part(dz)] if dz in (2, -2) else src.at[c]
            n = PIECES.index((dz, turn))
            out[dz, turn] = go(remote(
                at, into.at[part(dz), cols(0, y)], p_send.at[kind, n], p_recv.at[kind, n], device(-dz, at_y),
            ))
        return out

    back = {2: {}, 3: {}}
    far_first = (7, 3, 5, 6, 1, 2, 4, 0)
    for c in far_first:
        weights = pb[c] * (jnp.exp(tops[c] - largest) * share)
        pb[c] = weights
        grad = jnp.dot(weights.astype(jnp.bfloat16), gb[...], preferred_element_type=jnp.float32)
        dvb[c] = grad.astype(jnp.bfloat16)
        back[2].update(give(2, dvb, dvo, c))

    for copy in rd:
        copy.wait_recv()
    all_dots = [dots] + [take(rdi, i, 0) for i in range(3)]
    dots = functools.reduce(jnp.add, [d * r for d, r in zip(all_dots, scales)]) * share
    for c in range(8):
        sb[pl.ds(c * enc, enc), :] = (pb[c] * (wb[c] - dots)).astype(jnp.bfloat16)

    keys = kb[...].reshape(8 * enc, dim)
    dq_y = {}
    for e in (2, 3, 1):
        dqb[e] = tn(sb[:, e * block : (e + 1) * block], keys).astype(jnp.bfloat16)
        dq_y[e] = go(remote(dqb.at[e], dqy.at[e], y_send.at[2, e], y_recv.at[2, e], ypeer(NY - e)))

    for c in far_first:
        grad = jnp.dot(sb[pl.ds(c * enc, enc), :], qb[...], preferred_element_type=jnp.float32)
        dkb[c] = grad.astype(jnp.bfloat16)
        back[3].update(give(3, dkb, dko, c))

    mine = tn(sb[:, 0:block], keys)
    for e in range(1, NY):
        dq_y[e].wait_recv()
    mine = (mine + dqy[2].astype(jnp.float32)).astype(jnp.bfloat16)
    theirs = (dqy[1].astype(jnp.float32) + dqy[3].astype(jnp.float32)).astype(jnp.bfloat16)
    dqz[:, half_of(y)] = mine
    dqz[:, half_of(other)] = theirs
    dq_z = {
        d: go(remote(
            dqz.at[pl.ds(d * rows, rows)], dqr.at[d], z_send.at[2, d], z_recv.at[2, d], zpeer(NZ - d),
        ))
        for d in NEAR
    }
    dqr[0] = dqz[0:rows, :]

    for copy in back[2].values():
        copy.wait_recv()
    out_v = pltpu.make_async_copy(dvo, dv_ref, own.at[4])
    out_v.start()
    for copy in back[3].values():
        copy.wait_recv()
    out_k = pltpu.make_async_copy(dko, dk_ref, own.at[5])
    out_k.start()
    for d in range(1, NZ):
        dq_z[d].wait_recv()
    for d in range(GZ):
        dqo[:, pair(d)] = (dqr[d].astype(jnp.float32) + dqr[d + GZ].astype(jnp.float32)).astype(jnp.bfloat16)
    out_q = pltpu.make_async_copy(dqo, dq_ref, own.at[6])
    out_q.start()
    for copy in started:
        copy.wait_send()
    for copy in (out_v, out_k, out_q):
        copy.wait()


def settle(dq_from, dk_from, dv_from, dq_ref, dk_ref, dv_ref, dqm, dkm, dvm, sem):
    ins = [
        pltpu.make_async_copy(src, dst, sem.at[0, i])
        for i, (src, dst) in enumerate(((dk_from, dkm), (dv_from, dvm), (dq_from, dqm)))
    ]
    outs = [
        pltpu.make_async_copy(src, dst, sem.at[1, i])
        for i, (src, dst) in enumerate(((dkm, dk_ref), (dvm, dv_ref), (dqm, dq_ref)))
    ]
    for copy in ins:
        copy.start()
    for copy, out in zip(ins, outs):
        copy.wait()
        out.start()
    for out in outs:
        out.wait()


def body(queries, enc_keys, enc_values, grad_context, enc_lengths):
    rows, width = queries.shape[1:]
    enc = enc_keys.shape[1]
    dim = width // HEADS
    block = NZ * rows
    dec = NY * block
    lanes = dec // NY
    any_spec = pl.BlockSpec(memory_space=pl.ANY)
    bf16, f32 = jnp.bfloat16, jnp.float32
    vmem = pltpu.VMEM
    dma = pltpu.SemaphoreType.DMA
    outs = (
        jax.ShapeDtypeStruct((rows, width), bf16),
        jax.ShapeDtypeStruct((enc, width), bf16),
        jax.ShapeDtypeStruct((enc, width), bf16),
    )
    grads = pl.pallas_call(
        kernel,
        out_shape=outs,
        in_specs=[pl.BlockSpec(memory_space=pltpu.SMEM)] + [any_spec] * 4,
        out_specs=(any_spec,) * 3,
        scratch_shapes=[
            vmem((rows, width), bf16), vmem((enc, width), bf16),
            vmem((enc, width), bf16), vmem((rows, width), bf16),
            vmem((rows, width), bf16), vmem((enc, width), bf16), vmem((enc, width), bf16),
            vmem((block, 2 * dim), bf16), vmem((block, 2 * dim), bf16),
            vmem((dec, dim), bf16), vmem((dec, dim), bf16),
            vmem((8, enc, dim), bf16), vmem((8, enc, dim), bf16),
            vmem((8, enc, dec), f32), vmem((8, enc, dec), f32),
            vmem((8 * enc, dec), bf16),
            vmem((8, enc, dim), bf16), vmem((8, enc, dim), bf16),
            vmem((NY, block, dim), bf16), vmem((NY, block, dim), bf16),
            vmem((block, 2 * dim), bf16), vmem((NZ, rows, 2 * dim), bf16),
            vmem((2 * NY, lanes), f32), vmem((3, 2 * NY, lanes), f32),
            vmem((2 * NY, lanes), f32), vmem((3, 2 * NY, lanes), f32),
            dma((3, NZ)), dma((3, NZ)), dma((3, NY)), dma((3, NY)),
            dma((4, len(PIECES))), dma((4, len(PIECES))), dma((2, 3)), dma((2, 3)), dma((7,)),
        ],
        compiler_params=pltpu.CompilerParams(
            collective_id=0, has_side_effects=True, vmem_limit_bytes=56 * 1024 * 1024
        ),
        cost_estimate=pl.CostEstimate(
            flops=80 * enc * dec * dim,
            bytes_accessed=8 * enc * width + 6 * rows * width,
            transcendentals=8 * enc * dec,
        ),
    )(enc_lengths, queries[0], enc_keys[0], enc_values[0], grad_context[0])
    dq, dk, dv = pl.pallas_call(
        settle,
        out_shape=outs,
        in_specs=[any_spec] * 3,
        out_specs=(any_spec,) * 3,
        scratch_shapes=[vmem(a.shape, bf16) for a in outs] + [dma((2, 3))],
        compiler_params=pltpu.CompilerParams(vmem_limit_bytes=56 * 1024 * 1024),
    )(*grads)
    return (dq[None], dk[None], dv[None])


def solution(mesh):
    spec = P("dp", "seq", None)
    return jax.shard_map(
        body,
        mesh=mesh,
        in_specs=(spec, spec, spec, spec, P("dp")),
        out_specs=(spec, spec, spec),
        check_vma=False,
    )
```

```python
import functools

import jax
import jax.numpy as jnp
from jax import lax
from jax.experimental import pallas as pl
from jax.experimental.pallas import tpu as pltpu
from jax.sharding import PartitionSpec as P

HEADS = 8
NZ = 8
NY = 4
GZ = 4
MESH = pl.DeviceIdType.MESH
DEAD = -1e30
FLOOR = -1e20
PIECES = ((2, 1), (-2, 1), (1, 1), (-1, 1), (2, 0), (-2, 0), (1, 0), (-1, 0), (0, 1))
CHUNK = {0: 0, 1: 1, -1: 2, 2: 3, -2: 3}
NEAR = (4, 3, 5, 2, 6, 1, 7)


def nt(a, b):
    return lax.dot_general(a, b, (((1,), (1,)), ((), ())), preferred_element_type=jnp.float32)


def tn(a, b):
    return lax.dot_general(a, b, (((0,), (0,)), ((), ())), preferred_element_type=jnp.float32)


def kernel(
    len_ref, q_hbm, k_hbm, v_hbm, g_hbm,
    dq_ref, dk_ref, dv_ref,
    q_ref, k_ref, v_ref, g_ref, dqo, dko, dvo,
    qs, q1, gz, qb, gb, kb, vb, pb, wb, sb, dkb, dvb, dqb, dqy, dqz, dqr, mlo, mli, rdo, rdi,
    z_send, z_recv, y_send, y_recv, p_send, p_recv, s_send, s_recv, own,
):
    seq = lax.axis_index("seq")
    z, y = seq // NY, seq % NY
    rows = q_ref.shape[0]
    enc = k_ref.shape[0]
    dim = kb.shape[2]
    block = NZ * rows
    dec = NY * block
    lanes = mlo.shape[1]
    half = enc // 2
    side = y % 2
    other = y + 1 - 2 * side

    def device(dz, at_y):
        return ((z + dz + NZ) % NZ) * NY + at_y

    def zpeer(d):
        return device(d, y)

    def ypeer(e):
        return z * NY + (y + e) % NY

    def cols(dz, at_y):
        head = 2 * ((z + dz + NZ) % GZ) + at_y % 2
        return pl.ds(pl.multiple_of(head * dim, dim), dim)

    def pair(dz):
        return pl.ds(pl.multiple_of(((z + dz + NZ) % GZ) * (2 * dim), 2 * dim), 2 * dim)

    def half_of(at_y):
        return pl.ds(pl.multiple_of((at_y % 2) * dim, dim), dim)

    def part(dz):
        return {2: pl.ds(0, half), -2: pl.ds(half, half)}.get(dz, pl.ds(0, enc))

    def remote(src, dst, send, recv, peer):
        return pltpu.make_async_remote_copy(
            src_ref=src, dst_ref=dst, send_sem=send, recv_sem=recv,
            device_id={"seq": peer}, device_id_type=MESH,
        )

    started = []

    def go(copy):
        copy.start()
        started.append(copy)
        return copy

    loads = [
        pltpu.make_async_copy(src, dst, own.at[i])
        for i, (src, dst) in enumerate(((q_hbm, q_ref), (g_hbm, g_ref), (k_hbm, k_ref), (v_hbm, v_ref)))
    ]
    for copy in loads:
        copy.start()

    barrier = pltpu.get_barrier_semaphore()
    peers = [zpeer(d) for d in range(1, NZ)] + [ypeer(e) for e in range(1, NY)]
    peers += [device(dz, other) for dz in (1, -1, 2, -2)] + [device(4, (y + 2) % NY)]
    for peer in peers:
        pl.semaphore_signal(barrier, inc=1, device_id={"seq": peer}, device_id_type=MESH)
    pl.semaphore_wait(barrier, len(peers))

    def z_out(kind, src, into):
        return {
            d: go(remote(
                src.at[:, pair(d)], into.at[pl.ds(d * rows, rows)], z_send.at[kind, d], z_recv.at[kind, d], zpeer(d),
            ))
            for d in NEAR
        }

    def y_out(kind, src, into):
        return {
            e: go(remote(
                src.at[:, half_of(y + e)], into.at[pl.ds(e * block, block)],
                y_send.at[kind, e], y_recv.at[kind, e], ypeer(e),
            ))
            for e in (2, 3, 1)
        }

    def q_turn():
        return {
            d: go(remote(
                q1.at[:, (z + d) % GZ], qb.at[:, d], z_send.at[0, d], z_recv.at[0, d], zpeer(d),
            ))
            for d in NEAR
        }

    def p_out(kind, src, into):
        out = {}
        for i, (dz, turn) in enumerate(PIECES):
            at_y = other if turn else y
            at = into.at[4 * turn + CHUNK[dz], part(dz)] if dz in (2, -2) else into.at[4 * turn + CHUNK[dz]]
            out[dz, turn] = go(remote(
                src.at[part(dz), cols(dz, at_y)], at, p_send.at[kind, i], p_recv.at[kind, i], device(dz, at_y),
            ))
        return out

    loads[1].wait()
    g_in = z_out(1, g_ref, gz)
    loads[0].wait()
    for h in range(HEADS):
        qs[h % 2, h // 2] = q_ref[:, h * dim : (h + 1) * dim]
    q_in = {
        e: go(remote(qs.at[(y + e) % 2], q1.at[e], y_send.at[0, e], y_recv.at[0, e], ypeer(e)))
        for e in (2, 3, 1)
    }
    loads[2].wait()
    loads[3].wait()
    q1[0] = qs[side]
    gz[0:rows, :] = g_ref[:, pair(0)]
    for e in range(1, NY):
        q_in[e].wait_recv()
    q_all = q_turn()
    for d in reversed(NEAR):
        g_in[d].wait_recv()
    g_all = y_out(1, gz, gb)
    k_in = p_out(0, k_ref, kb)
    v_in = p_out(1, v_ref, vb)

    qb[:, 0] = q1[:, z % GZ]
    gb[0:block, :] = gz[:, half_of(y)]
    kb[0] = k_ref[:, cols(0, y)]
    vb[0] = v_ref[:, cols(0, y)]
    for d in reversed(NEAR):
        q_all[d].wait_recv()
    queries = qb[...].reshape(dec, dim)

    def arrive(copies, c):
        turn, i = divmod(c, 4)
        for dz in ((0,), (1,), (-1,), (2, -2))[i]:
            if (dz, turn) in copies:
                copies[dz, turn].wait_recv()

    order = (0, 4, 1, 2, 5, 6, 3, 7)

    length = len_ref[0]
    row = lax.broadcasted_iota(jnp.int32, (enc, dec), 0)
    tops, sums = [None] * 8, [None] * 8
    for c in order:
        arrive(k_in, c)
        turn, i = divmod(c, 4)
        at_y = other if turn else y

        def base(dz):
            return (((z + dz + NZ) % NZ) * NY + at_y) * enc

        first = (0, -1, 1, -2)[i]
        live = row + base(first) < length
        if i == 3:
            live = jnp.where(row < half, row + base(-2), row + base(2)) < length
        scores = jnp.where(live, nt(kb[c], queries), DEAD)
        top = jnp.maximum(jnp.max(scores, axis=0, keepdims=True), FLOOR)
        powers = jnp.exp(scores - top)
        tops[c], sums[c] = top, jnp.sum(powers, axis=0, keepdims=True)
        pb[c] = powers

    shared = (device(4, y), device(0, (y + 2) % NY), device(4, (y + 2) % NY))
    turned = ((4, 0), (0, 2), (4, 2))

    def put(buf, at, values):
        for i in range(NY):
            buf[at + i : at + i + 1, :] = values[:, i * lanes : (i + 1) * lanes]

    def exchange(kind, out, into):
        return [
            go(remote(out, into.at[i], s_send.at[kind, i], s_recv.at[kind, i], shared[i]))
            for i in range(3)
        ]

    def take(buf, i, at):
        tile = buf[i]
        if turned[i][0]:
            tile = pltpu.roll(tile, lanes // 2, 1)
        return jnp.concatenate(
            [tile[at + (k + turned[i][1]) % NY : at + (k + turned[i][1]) % NY + 1, :] for k in range(NY)], axis=1
        )

    top = functools.reduce(jnp.maximum, tops)
    total = functools.reduce(jnp.add, [s * jnp.exp(t - top) for s, t in zip(sums, tops)])
    put(mlo, 0, top)
    put(mlo, NY, total)
    ml = exchange(0, mlo, mli)
    for e in range(1, NY):
        g_all[e].wait_recv()

    dots = jnp.zeros((1, dec), jnp.float32)
    for c in order:
        arrive(v_in, c)
        weight_grad = nt(vb[c], gb[...])
        wb[c] = weight_grad
        dots = dots + jnp.sum(pb[c] * weight_grad, axis=0, keepdims=True) * jnp.exp(tops[c] - top)
    rdo[...] = jnp.zeros_like(rdo)
    put(rdo, 0, dots)
    rd = exchange(1, rdo, rdi)

    for copy in ml:
        copy.wait_recv()
    all_tops = [top] + [take(mli, i, 0) for i in range(3)]
    all_sums = [total] + [take(mli, i, NY) for i in range(3)]
    largest = functools.reduce(jnp.maximum, all_tops)
    scales = [jnp.exp(t - largest) for t in all_tops]
    share = 1.0 / functools.reduce(jnp.add, [s * r for s, r in zip(all_sums, scales)])

    def give(kind, src, into, c):
        turn, i = divmod(c, 4)
        out = {}
        for dz in ((0,), (1,), (-1,), (2, -2))[i]:
            if (dz, turn) not in PIECES:
                into[:, cols(0, y)] = src[c]
                continue
            at_y = other if turn else y
            at = src.at[c, part(dz)] if dz in (2, -2) else src.at[c]
            n = PIECES.index((dz, turn))
            out[dz, turn] = go(remote(
                at, into.at[part(dz), cols(0, y)], p_send.at[kind, n], p_recv.at[kind, n], device(-dz, at_y),
            ))
        return out

    back = {2: {}, 3: {}}
    far_first = (7, 3, 5, 6, 1, 2, 4, 0)
    for c in far_first:
        weights = pb[c] * (jnp.exp(tops[c] - largest) * share)
        pb[c] = weights
        grad = jnp.dot(weights.astype(jnp.bfloat16), gb[...], preferred_element_type=jnp.float32)
        dvb[c] = grad.astype(jnp.bfloat16)
        back[2].update(give(2, dvb, dvo, c))

    for copy in rd:
        copy.wait_recv()
    all_dots = [dots] + [take(rdi, i, 0) for i in range(3)]
    dots = functools.reduce(jnp.add, [d * r for d, r in zip(all_dots, scales)]) * share
    for c in range(8):
        sb[pl.ds(c * enc, enc), :] = (pb[c] * (wb[c] - dots)).astype(jnp.bfloat16)

    keys = kb[...].reshape(8 * enc, dim)
    dq_y = {}
    for e in (2, 3, 1):
        dqb[e] = tn(sb[:, e * block : (e + 1) * block], keys).astype(jnp.bfloat16)
        dq_y[e] = go(remote(dqb.at[e], dqy.at[e], y_send.at[2, e], y_recv.at[2, e], ypeer(NY - e)))

    for c in far_first:
        grad = jnp.dot(sb[pl.ds(c * enc, enc), :], qb[...].reshape(dec, dim), preferred_element_type=jnp.float32)
        dkb[c] = grad.astype(jnp.bfloat16)
        back[3].update(give(3, dkb, dko, c))

    mine = tn(sb[:, 0:block], keys)
    for e in range(1, NY):
        dq_y[e].wait_recv()
    mine = (mine + dqy[2].astype(jnp.float32)).astype(jnp.bfloat16)
    theirs = (dqy[1].astype(jnp.float32) + dqy[3].astype(jnp.float32)).astype(jnp.bfloat16)
    dqz[:, half_of(y)] = mine
    dqz[:, half_of(other)] = theirs
    dq_z = {
        d: go(remote(
            dqz.at[pl.ds(d * rows, rows)], dqr.at[d], z_send.at[2, d], z_recv.at[2, d], zpeer(NZ - d),
        ))
        for d in NEAR
    }
    dqr[0] = dqz[0:rows, :]

    for copy in back[2].values():
        copy.wait_recv()
    out_v = pltpu.make_async_copy(dvo, dv_ref, own.at[4])
    out_v.start()
    for copy in back[3].values():
        copy.wait_recv()
    out_k = pltpu.make_async_copy(dko, dk_ref, own.at[5])
    out_k.start()
    for d in range(1, NZ):
        dq_z[d].wait_recv()
    for d in range(GZ):
        dqo[:, pair(d)] = (dqr[d].astype(jnp.float32) + dqr[d + GZ].astype(jnp.float32)).astype(jnp.bfloat16)
    out_q = pltpu.make_async_copy(dqo, dq_ref, own.at[6])
    out_q.start()
    for copy in started:
        copy.wait_send()
    for copy in (out_v, out_k, out_q):
        copy.wait()


def settle(dq_from, dk_from, dv_from, dq_ref, dk_ref, dv_ref, dqm, dkm, dvm, sem):
    ins = [
        pltpu.make_async_copy(src, dst, sem.at[0, i])
        for i, (src, dst) in enumerate(((dk_from, dkm), (dv_from, dvm), (dq_from, dqm)))
    ]
    outs = [
        pltpu.make_async_copy(src, dst, sem.at[1, i])
        for i, (src, dst) in enumerate(((dkm, dk_ref), (dvm, dv_ref), (dqm, dq_ref)))
    ]
    for copy in ins:
        copy.start()
    for copy, out in zip(ins, outs):
        copy.wait()
        out.start()
    for out in outs:
        out.wait()


def body(queries, enc_keys, enc_values, grad_context, enc_lengths):
    rows, width = queries.shape[1:]
    enc = enc_keys.shape[1]
    dim = width // HEADS
    block = NZ * rows
    dec = NY * block
    lanes = dec // NY
    any_spec = pl.BlockSpec(memory_space=pl.ANY)
    bf16, f32 = jnp.bfloat16, jnp.float32
    vmem = pltpu.VMEM
    dma = pltpu.SemaphoreType.DMA
    outs = (
        jax.ShapeDtypeStruct((rows, width), bf16),
        jax.ShapeDtypeStruct((enc, width), bf16),
        jax.ShapeDtypeStruct((enc, width), bf16),
    )
    grads = pl.pallas_call(
        kernel,
        out_shape=outs,
        in_specs=[pl.BlockSpec(memory_space=pltpu.SMEM)] + [any_spec] * 4,
        out_specs=(any_spec,) * 3,
        scratch_shapes=[
            vmem((rows, width), bf16), vmem((enc, width), bf16),
            vmem((enc, width), bf16), vmem((rows, width), bf16),
            vmem((rows, width), bf16), vmem((enc, width), bf16), vmem((enc, width), bf16),
            vmem((2, GZ, rows, dim), bf16), vmem((NY, GZ, rows, dim), bf16), vmem((block, 2 * dim), bf16),
            vmem((NY, NZ, rows, dim), bf16), vmem((dec, dim), bf16),
            vmem((8, enc, dim), bf16), vmem((8, enc, dim), bf16),
            vmem((8, enc, dec), f32), vmem((8, enc, dec), f32),
            vmem((8 * enc, dec), bf16),
            vmem((8, enc, dim), bf16), vmem((8, enc, dim), bf16),
            vmem((NY, block, dim), bf16), vmem((NY, block, dim), bf16),
            vmem((block, 2 * dim), bf16), vmem((NZ, rows, 2 * dim), bf16),
            vmem((2 * NY, lanes), f32), vmem((3, 2 * NY, lanes), f32),
            vmem((2 * NY, lanes), f32), vmem((3, 2 * NY, lanes), f32),
            dma((3, NZ)), dma((3, NZ)), dma((3, NY)), dma((3, NY)),
            dma((4, len(PIECES))), dma((4, len(PIECES))), dma((2, 3)), dma((2, 3)), dma((7,)),
        ],
        compiler_params=pltpu.CompilerParams(
            collective_id=0, has_side_effects=True, vmem_limit_bytes=56 * 1024 * 1024
        ),
        cost_estimate=pl.CostEstimate(
            flops=80 * enc * dec * dim,
            bytes_accessed=8 * enc * width + 6 * rows * width,
            transcendentals=8 * enc * dec,
        ),
    )(enc_lengths, queries[0], enc_keys[0], enc_values[0], grad_context[0])
    dq, dk, dv = pl.pallas_call(
        settle,
        out_shape=outs,
        in_specs=[any_spec] * 3,
        out_specs=(any_spec,) * 3,
        scratch_shapes=[vmem(a.shape, bf16) for a in outs] + [dma((2, 3))],
        compiler_params=pltpu.CompilerParams(vmem_limit_bytes=56 * 1024 * 1024),
    )(*grads)
    return (dq[None], dk[None], dv[None])


def solution(mesh):
    spec = P("dp", "seq", None)
    return jax.shard_map(
        body,
        mesh=mesh,
        in_specs=(spec, spec, spec, spec, P("dp")),
        out_specs=(spec, spec, spec),
        check_vma=False,
    )
```
